256 devices in a mesh: row: 16 (over y, x), col: 8 (over z), layer: 2 (over core).
Axes of the slice: x: 4, y: 4, z: 8, core: 2. Of those that a mesh axis runs over, the one named last changes fastest.
Arguments:
- density: bfloat16 [4096, 4096], P('row', 'col'), may hold values from -0.125 to 0.125
- panel: bfloat16 [4096, 16384], P('row', 'col'), may hold values from -6 to 6
- pattern: int32 [32, 32], P('row', 'col'), may hold values 0 or 1
Outputs:
- purified: bfloat16 [4096, 16384], P('row', ('col', 'layer'))
The draws below stay inside these ranges and needn't reach their ends.
All inputs are finite; a program needn't handle non-finite values. No bound on the sum of `pattern` on one device may be relied on, other than what follows from the above.
Results may differ from the reference program's by a relative error of at most 0.0034.
Values may be sent and summed in bfloat16 or wider, within the bound.
No kernel may reach another device: no remote copies, remote signals or barrier semaphores. Data moves between devices by JAX's collectives and lax.ppermute only.
A program may use at most 64 MiB of HBM per device.

```python
import jax
import jax.numpy as jnp

BS = 128
NB = 32
K = 4096
PW = 16384


def with_ends(drawn, key, smallest, high):
    index_at = [jax.random.randint(jax.random.fold_in(key, axis), (), 0, length) for axis, length in enumerate(drawn.shape)]
    longest = drawn.shape.index(max(drawn.shape))
    neighbour = index_at[:longest] + [(index_at[longest] + 1) % drawn.shape[longest]] + index_at[longest + 1:]
    return drawn.at[tuple(index_at)].set(smallest).at[tuple(neighbour)].set(high)


def levels(stream_key, dims, pieces, smallest, top_value):
    loudness, own = 1.0, jax.random.fold_in(stream_key, 6)
    for axis_at, shards_of in pieces:
        draws = jnp.exp(jax.random.uniform(jax.random.fold_in(own, axis_at), (shards_of,), jnp.float32, smallest / len(pieces), top_value / len(pieces)))
        loudness = loudness * jnp.repeat(draws, dims[axis_at] // shards_of).reshape([-1 if axis == axis_at else 1 for axis in range(len(dims))])
    return loudness


def scatter_about(own_key, extent, deviation, most, shards=(), kind=jnp.bfloat16):
    result = jax.random.normal(own_key, extent, jnp.float32) * deviation
    if len(shards) > 0:
        result = levels(own_key, extent, shards, -0.22, 0.18) * result
    return jnp.clip(result, min=-most, max=most).astype(kind)


def setup_inputs(seed: int = 0) -> dict:
    key_of = jax.random.split(jax.random.key(seed), 4)
    density = scatter_about(key_of[0], (K, K), (K // 2) ** -0.5, 0.125, ((0, 16), (1, 8)))
    panel = scatter_about(key_of[1], (K, PW), 1.0, 6.0, ((0, 16), (1, 8)))
    pattern = with_ends((jax.random.randint(key_of[2], (NB, NB), 0, 2) < 1).astype(jnp.int32), jax.random.fold_in(key_of[2], 1), 0, 1)
    return dict(density=density, panel=panel, pattern=pattern)


def reference(density, panel, pattern):
    expanded = jnp.repeat(jnp.repeat(pattern, BS, axis=0), BS, axis=1).astype(jnp.bfloat16)
    filtered = density * expanded
    square = jnp.dot(filtered, panel, preferred_element_type=jnp.float32)
    square_low = square.astype(jnp.bfloat16)
    cubic = jnp.dot(filtered, square_low, preferred_element_type=jnp.float32)
    return (3.0 * square - 2.0 * cubic).astype(jnp.bfloat16)
```

```python
import jax
import jax.numpy as jnp
from jax import lax
from jax.experimental import pallas as pl
from jax.experimental.pallas import tpu as pltpu
from jax.sharding import Mesh, PartitionSpec as P

BS = 128
NY, NX, NZ, NC = 4, 4, 8, 2
ROWS, INNER = 256, 512
HALF = NZ // 2
BF16, F32 = jnp.bfloat16, jnp.float32


def row_routes():
    routes = []
    for k in range(HALF):
        route = []
        for z in range(NZ):
            for c in range(NC):
                source = (HALF * c + (z + k) % HALF) * NC + z // HALF
                route.append((source, z * NC + c))
        routes.append(route)
    return routes


def column_routes():
    routes = []
    for i in range(2):
        for j in range(NX):
            route = []
            for y in range(NY):
                for x in range(NX):
                    for c in range(NC):
                        source_y, source_x = 2 * c + (y + i) % 2, (x + j) % NX
                        source = (source_y * NX + source_x) * NC + y // 2
                        route.append((source, (y * NX + x) * NC + c))
            routes.append(route)
    return routes


SWAP = [(0, 1), (1, 0)]


def square_kernel(place, *refs):
    row_refs, col_refs = refs[:HALF], refs[HALF : HALF + 2 * NX]
    out_ref, left, right = refs[HALF + 2 * NX :]
    y, x, z = place[0], place[1], place[2]
    for k in range(HALF):
        at = pl.multiple_of((z + k) % HALF * INNER, INNER)
        left[:, pl.ds(at, INNER)] = row_refs[k][...]
    for i in range(2):
        for j in range(NX):
            at = pl.multiple_of(((y + i) % 2 * NX + (x + j) % NX) * ROWS, ROWS)
            right[pl.ds(at, ROWS), :] = col_refs[i * NX + j][...]
    out_ref[...] = jnp.dot(left[...], right[...], preferred_element_type=F32)


def partial_square(place, rows, cols):
    vmem = pl.BlockSpec(memory_space=pltpu.VMEM)
    return pl.pallas_call(
        square_kernel,
        out_shape=jax.ShapeDtypeStruct((ROWS, INNER), F32),
        in_specs=[pl.BlockSpec(memory_space=pltpu.SMEM)] + [vmem] * (len(rows) + len(cols)),
        out_specs=vmem,
        scratch_shapes=[
            pltpu.VMEM((ROWS, HALF * INNER), BF16),
            pltpu.VMEM((HALF * INNER, INNER), BF16),
        ],
        compiler_params=pltpu.CompilerParams(vmem_limit_bytes=32 * 1024 * 1024),
        cost_estimate=pl.CostEstimate(
            flops=2 * ROWS * INNER * HALF * INNER, bytes_accessed=4 << 20, transcendentals=0
        ),
    )(place, *rows, *cols)


def gather_rows(block):
    return [lax.ppermute(block, ("z", "c"), route) for route in row_routes()]


def assemble(own, core, z):
    other = lax.ppermute(jnp.concatenate(own, 1), "c", SWAP)
    mine = jnp.concatenate(own, 1)
    start = (HALF - z % HALF) % HALF * INNER

    def in_place(part):
        return lax.dynamic_slice_in_dim(
            jnp.concatenate([part, part], 1), start, HALF * INNER, 1
        )

    mine, other = in_place(mine), in_place(other)
    return jnp.where(
        core == 0,
        jnp.concatenate([mine, other], 1),
        jnp.concatenate([other, mine], 1),
    )


def shards(density, panel, pattern):
    y, x, z, core = (lax.axis_index(name) for name in ("y", "x", "z", "c"))
    mask = pattern.astype(BF16)
    filtered = (
        density.reshape(ROWS // BS, BS, INNER // BS, BS) * mask[:, None, :, None]
    ).reshape(ROWS, INNER)
    width = panel.shape[1] // NC
    mine = lax.dynamic_slice_in_dim(panel, core * width, width, 1)
    panel_cols = lax.all_gather(mine, ("y", "x"), axis=0, tiled=True)

    rows = gather_rows(filtered)
    cols = [lax.ppermute(filtered, ("y", "x", "c"), route) for route in column_routes()]
    place = jnp.stack([y, x, z]).astype(jnp.int32)
    part = partial_square(place, rows, cols)
    squared = (part + lax.ppermute(part, "c", SWAP)).astype(BF16)
    squared_rows = assemble(gather_rows(squared), core, z)
    filtered_rows = assemble(rows, core, z)
    first = jnp.dot(filtered_rows, panel_cols, preferred_element_type=F32)
    second = jnp.dot(squared_rows, panel_cols, preferred_element_type=F32)
    return (3.0 * first - 2.0 * second).astype(BF16)


def solution(mesh):
    fine = Mesh(mesh.devices.reshape(NY, NX, NZ, NC), ("y", "x", "z", "c"))
    rows = ("y", "x")
    return jax.shard_map(
        shards,
        mesh=fine,
        in_specs=(P(rows, "z"), P(rows, "z"), P(rows, "z")),
        out_specs=P(rows, ("z", "c")),
        check_vma=False,
    )
```

```python
import functools

import jax
import jax.numpy as jnp
from jax import lax
from jax.experimental import pallas as pl
from jax.experimental.pallas import tpu as pltpu
from jax.sharding import Mesh, PartitionSpec as P

BS = 128
NY, NX, NZ, NC = 4, 4, 8, 2
ROWS, INNER, WIDTH = 256, 512, 1024
PART = INNER // NC
DEPTH = NY * NX * ROWS
AXES = ("y", "x", "z", "c")
BF16, F32 = jnp.bfloat16, jnp.float32


def moved(block, source_of):
    def index(y, x, z, c):
        return ((y * NX + x) * NZ + z) * NC + c

    route = []
    for y in range(NY):
        for x in range(NX):
            for z in range(NZ):
                for c in range(NC):
                    source = source_of(y, x, z, c)
                    if source is not None:
                        route.append((index(*source), index(y, x, z, c)))
    return lax.ppermute(block, AXES, route)


def first(block, step):
    return moved(
        block,
        lambda y, x, z, c: ((y + step) % NY, x, z, c) if c == 0 else (y, (x + step) % NX, z, c),
    )


def second(block, step):
    return moved(
        block,
        lambda y, x, z, c: (y, (x + step) % NX, z, c) if c == 0 else ((y + step) % NY, x, z, c),
    )


def swapped(block):
    return moved(block, lambda y, x, z, c: (y, x, z, 1 - c))


def along(block, step):
    return moved(block, lambda y, x, z, c: (y, x, (z + (step if c == 0 else -step)) % NZ, c))


def joined(blocks):
    return jnp.stack(blocks)


def after(value, *others):
    return lax.optimization_barrier((value, others))[0]


def farther(two_on):
    four = moved(two_on, lambda y, x, z, c: (y, x, (z + 2) % NZ, c) if c == 0 else None)
    return along(two_on, 1), four


def positions():
    y, x, z, c = (lax.axis_index(name) for name in AXES)

    def place(offset, half):
        block = 2 * ((z + offset + NZ) % NZ) + half
        down, right = (block // NX - y + NY) % NY, (block % NX - x + NX) % NX
        d = jnp.where(c == 0, down, right)
        e = jnp.where(c == 0, right, down)
        return pl.multiple_of((e * NY + d) * ROWS, ROWS)

    return c, place


def reorder(own_ref, mine_ref, other_ref, out_ref, halves):
    c, place = positions()
    way = 1 - 2 * c
    for h in range(2):
        out_ref[:, pl.ds(place(0, halves(c, h)), ROWS)] = own_ref(h)
        for k in range(3):
            out_ref[:, pl.ds(place(way * (k + 1), halves(c, h)), ROWS)] = mine_ref(k, h)
            out_ref[:, pl.ds(place(-way * (k + 1), halves(1 - c, h)), ROWS)] = other_ref(k, h)
        far = place(4, halves(0, h))

        @pl.when(c == 0)
        def _():
            out_ref[:, pl.ds(far, ROWS)] = mine_ref(3, h)

        @pl.when(c == 1)
        def _():
            out_ref[:, pl.ds(far, ROWS)] = other_ref(3, h)


def contract(row_ref, places, stacks):
    total = None
    for (e, d), ref in zip(places, stacks):
        count = ref.shape[0] * ROWS
        at = (e * NY + d) * ROWS
        panel = ref[...].reshape(count, ref.shape[2])
        term = jnp.dot(row_ref[:, at : at + count], panel, preferred_element_type=F32)
        total = term if total is None else total + term
    return total


def square_kernel(places, own, mine, other, *refs):
    stacks, (row_ref, out_ref) = refs[: len(places)], refs[len(places) :]

    def half(h):
        return slice(h * ROWS, (h + 1) * ROWS)

    reorder(
        lambda h: own[:, half(h)],
        lambda k, h: mine[k, :, half(h)],
        lambda k, h: other[k, :, half(h)],
        row_ref,
        lambda core, h: h,
    )
    out_ref[...] = contract(row_ref, places, stacks).astype(BF16)


def single_kernel(places, row_ref, *refs):
    stacks, (out_ref,) = refs[: len(places)], refs[len(places) :]
    out_ref[...] = contract(row_ref, places, stacks)


def final_kernel(places, own, mine, other, one, *refs):
    stacks, (out_ref, row_ref) = refs[: len(places)], refs[len(places) :]
    reorder(
        lambda h: own[h],
        lambda k, h: mine[k, h],
        lambda k, h: other[k, h],
        row_ref,
        lambda core, h: core if h == 0 else 1 - core,
    )
    two = contract(row_ref, places, stacks)
    out_ref[...] = (3.0 * one[...] - 2.0 * two).astype(BF16)


def call(kernel, out_shape, scratch, flops, *operands):
    vmem = pl.BlockSpec(memory_space=pltpu.VMEM)
    return pl.pallas_call(
        kernel,
        out_shape=out_shape,
        in_specs=[vmem] * len(operands),
        out_specs=jax.tree.map(lambda _: vmem, out_shape),
        scratch_shapes=scratch,
        compiler_params=pltpu.CompilerParams(vmem_limit_bytes=16 * 1024 * 1024),
        cost_estimate=pl.CostEstimate(flops=flops, bytes_accessed=1 << 20, transcendentals=0),
    )(*operands)


def shards(density, panel, pattern):
    core = lax.axis_index("c")
    mask = pattern.astype(BF16)
    filtered = (
        density.reshape(ROWS // BS, BS, INNER // BS, BS) * mask[:, None, :, None]
    ).reshape(ROWS, INNER)
    own_columns = lax.dynamic_slice_in_dim(filtered, core * PART, PART, 1)
    own_panel = lax.dynamic_slice_in_dim(panel, core * WIDTH, WIDTH, 1)

    both = jnp.concatenate([own_columns, own_panel], 1)
    near = [both] + [first(both, d) for d in (1, 2, 3)]
    one_on, two_on = along(filtered, 1), along(filtered, 2)
    near_columns = joined([block[:, :PART] for block in near])
    near_panel = joined([block[:, PART:] for block in near])

    near_columns = after(near_columns, one_on, two_on)
    two_tied = after(two_on, *near[1:])
    columns = [near_columns] + [second(near_columns, e) for e in (1, 2, 3)]
    filtered_mine = joined([one_on, two_on, *farther(two_tied)])
    filtered_mine = after(filtered_mine, *columns[1:])
    filtered_line = (filtered, filtered_mine, swapped(filtered_mine))

    near_panel = after(near_panel, *columns[1:])
    plus, minus = second(near_panel, 1), second(near_panel, 3)
    row, squared = call(
        functools.partial(square_kernel, [(e, 0) for e in range(NX)]),
        (jax.ShapeDtypeStruct((ROWS, DEPTH), BF16), jax.ShapeDtypeStruct((ROWS, PART), BF16)),
        [],
        2 * ROWS * DEPTH * PART,
        *filtered_line,
        *columns,
    )
    squared = joined([squared, swapped(squared)])
    one_on, two_on = along(squared, 1), along(squared, 2)
    squared_mine = joined([one_on, two_on, *farther(two_on)])
    squared_mine = after(squared_mine, plus, minus)
    squared_line = (squared, squared_mine, swapped(squared_mine))
    parts = [
        (0, 0, near_panel),
        (1, 0, plus),
        (3, 0, minus),
        (2, 0, second(plus[:2], 1)),
        (2, 2, second(minus[2:], 3)),
    ]
    places, stacks = [(e, d) for e, d, _ in parts], [blocks for _, _, blocks in parts]
    one = call(
        functools.partial(single_kernel, places),
        jax.ShapeDtypeStruct((ROWS, WIDTH), F32),
        [],
        2 * ROWS * DEPTH * WIDTH,
        row,
        *stacks,
    )
    return call(
        functools.partial(final_kernel, places),
        jax.ShapeDtypeStruct((ROWS, WIDTH), BF16),
        [pltpu.VMEM((ROWS, DEPTH), BF16)],
        2 * ROWS * DEPTH * WIDTH,
        *squared_line,
        one,
        *stacks,
    )


def solution(mesh):
    fine = Mesh(mesh.devices.reshape(NY, NX, NZ, NC), AXES)
    rows = ("y", "x")
    return jax.shard_map(
        shards,
        mesh=fine,
        in_specs=(P(rows, "z"), P(rows, "z"), P(rows, "z")),
        out_specs=P(rows, ("z", "c")),
        check_vma=False,
    )
```

```python
import functools

import jax
import jax.numpy as jnp
from jax import lax
from jax.experimental import pallas as pl
from jax.experimental.pallas import tpu as pltpu
from jax.sharding import Mesh, PartitionSpec as P

BS = 128
NY, NX, NZ, NC = 4, 4, 8, 2
ROWS, INNER, WIDTH = 256, 512, 1024
PART = INNER // NC
DEPTH = NY * NX * ROWS
AXES = ("y", "x", "z", "c")
BF16, F32 = jnp.bfloat16, jnp.float32


def moved(block, source_of):
    def index(y, x, z, c):
        return ((y * NX + x) * NZ + z) * NC + c

    route = []
    for y in range(NY):
        for x in range(NX):
            for z in range(NZ):
                for c in range(NC):
                    source = source_of(y, x, z, c)
                    if source is not None:
                        route.append((index(*source), index(y, x, z, c)))
    return lax.ppermute(block, AXES, route)


def first(block, step):
    return moved(
        block,
        lambda y, x, z, c: ((y + step) % NY, x, z, c) if c == 0 else (y, (x + step) % NX, z, c),
    )


def second(block, step):
    return moved(
        block,
        lambda y, x, z, c: (y, (x + step) % NX, z, c) if c == 0 else ((y + step) % NY, x, z, c),
    )


def swapped(block):
    return moved(block, lambda y, x, z, c: (y, x, z, 1 - c))


def along(block, step):
    return moved(block, lambda y, x, z, c: (y, x, (z + (step if c == 0 else -step)) % NZ, c))


def joined(blocks):
    return jnp.stack(blocks)


def after(value, *others):
    return lax.optimization_barrier((value, others))[0]


def farther(two_on):
    four = moved(two_on, lambda y, x, z, c: (y, x, (z + 2) % NZ, c) if c == 0 else None)
    return along(two_on, 1), four


def positions():
    y, x, z, c = (lax.axis_index(name) for name in AXES)

    def place(offset, half):
        block = 2 * ((z + offset + NZ) % NZ) + half
        down, right = (block // NX - y + NY) % NY, (block % NX - x + NX) % NX
        d = jnp.where(c == 0, down, right)
        e = jnp.where(c == 0, right, down)
        return pl.multiple_of((e * NY + d) * ROWS, ROWS)

    return c, place


def reorder(own_ref, mine_ref, other_ref, out_ref, halves):
    c, place = positions()
    way = 1 - 2 * c
    for h in range(2):
        out_ref[:, pl.ds(place(0, halves(c, h)), ROWS)] = own_ref(h)
        for k in range(3):
            out_ref[:, pl.ds(place(way * (k + 1), halves(c, h)), ROWS)] = mine_ref(k, h)
            out_ref[:, pl.ds(place(-way * (k + 1), halves(1 - c, h)), ROWS)] = other_ref(k, h)
        far = place(4, halves(0, h))

        @pl.when(c == 0)
        def _():
            out_ref[:, pl.ds(far, ROWS)] = mine_ref(3, h)

        @pl.when(c == 1)
        def _():
            out_ref[:, pl.ds(far, ROWS)] = other_ref(3, h)


def contract(row_ref, places, stacks):
    total = None
    for (e, d), ref in zip(places, stacks):
        count = ref.shape[0] * ROWS
        at = (e * NY + d) * ROWS
        panel = ref[...].reshape(count, ref.shape[2])
        term = jnp.dot(row_ref[:, at : at + count], panel, preferred_element_type=F32)
        total = term if total is None else total + term
    return total


def square_kernel(places, own, mine, other, *refs):
    stacks, (row_ref, out_ref) = refs[: len(places)], refs[len(places) :]

    def half(h):
        return slice(h * ROWS, (h + 1) * ROWS)

    reorder(
        lambda h: own[:, half(h)],
        lambda k, h: mine[k, :, half(h)],
        lambda k, h: other[k, :, half(h)],
        row_ref,
        lambda core, h: h,
    )
    out_ref[...] = contract(row_ref, places, stacks).astype(BF16)


def single_kernel(places, row_ref, *refs):
    stacks, (out_ref,) = refs[: len(places)], refs[len(places) :]
    out_ref[...] = contract(row_ref, places, stacks)


def final_kernel(places, own, mine, other, one, *refs):
    stacks, (out_ref, row_ref) = refs[: len(places)], refs[len(places) :]
    reorder(
        lambda h: own[h],
        lambda k, h: mine[k, h],
        lambda k, h: other[k, h],
        row_ref,
        lambda core, h: core if h == 0 else 1 - core,
    )
    two = contract(row_ref, places, stacks)
    out_ref[...] = (3.0 * one[...] - 2.0 * two).astype(BF16)


def call(kernel, out_shape, scratch, flops, *operands):
    vmem = pl.BlockSpec(memory_space=pltpu.VMEM)
    return pl.pallas_call(
        kernel,
        out_shape=out_shape,
        in_specs=[vmem] * len(operands),
        out_specs=jax.tree.map(lambda _: vmem, out_shape),
        scratch_shapes=scratch,
        compiler_params=pltpu.CompilerParams(vmem_limit_bytes=16 * 1024 * 1024),
        cost_estimate=pl.CostEstimate(flops=flops, bytes_accessed=1 << 20, transcendentals=0),
    )(*operands)


def shards(density, panel, pattern):
    core = lax.axis_index("c")
    mask = pattern.astype(BF16)
    filtered = (
        density.reshape(ROWS // BS, BS, INNER // BS, BS) * mask[:, None, :, None]
    ).reshape(ROWS, INNER)
    own_columns = lax.dynamic_slice_in_dim(filtered, core * PART, PART, 1)
    own_panel = lax.dynamic_slice_in_dim(panel, core * WIDTH, WIDTH, 1)

    both = jnp.concatenate([own_columns, own_panel], 1)
    both_one, both_three = first(both, 1), first(both, 3)
    columns_two = first(own_columns, 2)
    one_on, two_on = along(filtered, 1), along(filtered, 2)
    near_columns = joined([own_columns, both_one[:, :PART], columns_two, both_three[:, :PART]])

    near_columns = after(near_columns, one_on, two_on)
    pair = after(joined([one_on, two_on]), both_one, both_three, columns_two)
    panel_two = first(after(own_panel, both_one, both_three, columns_two), 2)
    near_panel = joined([own_panel, both_one[:, PART:], panel_two, both_three[:, PART:]])
    columns = [near_columns] + [second(near_columns, e) for e in (1, 2, 3)]
    filtered_mine = jnp.concatenate([pair, along(pair, 2)], 0)
    filtered_mine = after(filtered_mine, *columns[1:])
    filtered_line = (filtered, filtered_mine, swapped(filtered_mine))

    near_panel = after(near_panel, *columns[1:])
    plus, minus = second(near_panel, 1), second(near_panel, 3)
    row, squared = call(
        functools.partial(square_kernel, [(e, 0) for e in range(NX)]),
        (jax.ShapeDtypeStruct((ROWS, DEPTH), BF16), jax.ShapeDtypeStruct((ROWS, PART), BF16)),
        [],
        2 * ROWS * DEPTH * PART,
        *filtered_line,
        *columns,
    )
    squared = joined([squared, swapped(squared)])
    one_on, two_on = along(squared, 1), along(squared, 2)
    squared_mine = joined([one_on, two_on, *farther(two_on)])
    squared_mine = after(squared_mine, plus, minus)
    squared_line = (squared, squared_mine, swapped(squared_mine))
    parts = [
        (0, 0, near_panel),
        (1, 0, plus),
        (3, 0, minus),
        (2, 0, second(plus[:2], 1)),
        (2, 2, second(minus[2:], 3)),
    ]
    places, stacks = [(e, d) for e, d, _ in parts], [blocks for _, _, blocks in parts]
    one = call(
        functools.partial(single_kernel, places),
        jax.ShapeDtypeStruct((ROWS, WIDTH), F32),
        [],
        2 * ROWS * DEPTH * WIDTH,
        row,
        *stacks,
    )
    return call(
        functools.partial(final_kernel, places),
        jax.ShapeDtypeStruct((ROWS, WIDTH), BF16),
        [pltpu.VMEM((ROWS, DEPTH), BF16)],
        2 * ROWS * DEPTH * WIDTH,
        *squared_line,
        one,
        *stacks,
    )


def solution(mesh):
    fine = Mesh(mesh.devices.reshape(NY, NX, NZ, NC), AXES)
    rows = ("y", "x")
    return jax.shard_map(
        shards,
        mesh=fine,
        in_specs=(P(rows, "z"), P(rows, "z"), P(rows, "z")),
        out_specs=P(rows, ("z", "c")),
        check_vma=False,
    )
```

```python
import functools

import jax
import jax.numpy as jnp
from jax import lax
from jax.experimental import pallas as pl
from jax.experimental.pallas import tpu as pltpu
from jax.sharding import Mesh, PartitionSpec as P

BS = 128
NY, NX, NZ, NC = 4, 4, 8, 2
ROWS, INNER, WIDTH = 256, 512, 1024
PART = INNER // NC
DEPTH = NY * NX * ROWS
AXES = ("y", "x", "z", "c")
BF16, F32 = jnp.bfloat16, jnp.float32


def moved(block, source_of):
    def index(y, x, z, c):
        return ((y * NX + x) * NZ + z) * NC + c

    route = []
    for y in range(NY):
        for x in range(NX):
            for z in range(NZ):
                for c in range(NC):
                    source = source_of(y, x, z, c)
                    if source is not None:
                        route.append((index(*source), index(y, x, z, c)))
    return lax.ppermute(block, AXES, route)


def first(block, step):
    return moved(
        block,
        lambda y, x, z, c: ((y + step) % NY, x, z, c) if c == 0 else (y, (x + step) % NX, z, c),
    )


def second(block, step):
    return moved(
        block,
        lambda y, x, z, c: (y, (x + step) % NX, z, c) if c == 0 else ((y + step) % NY, x, z, c),
    )


def swapped(block):
    return moved(block, lambda y, x, z, c: (y, x, z, 1 - c))


def along(block, step):
    return moved(block, lambda y, x, z, c: (y, x, (z + (step if c == 0 else -step)) % NZ, c))


def joined(blocks):
    return jnp.stack(blocks)


def after(value, *others):
    return lax.optimization_barrier((value, others))[0]


def farther(two_on):
    four = moved(two_on, lambda y, x, z, c: (y, x, (z + 2) % NZ, c) if c == 0 else None)
    return along(two_on, 1), four


def positions():
    y, x, z, c = (lax.axis_index(name) for name in AXES)

    def place(offset, half):
        block = 2 * ((z + offset + NZ) % NZ) + half
        down, right = (block // NX - y + NY) % NY, (block % NX - x + NX) % NX
        d = jnp.where(c == 0, down, right)
        e = jnp.where(c == 0, right, down)
        return pl.multiple_of((e * NY + d) * ROWS, ROWS)

    return c, place


def reorder(own_ref, mine_ref, other_ref, out_ref, halves):
    c, place = positions()
    way = 1 - 2 * c
    for h in range(2):
        out_ref[:, pl.ds(place(0, halves(c, h)), ROWS)] = own_ref(h)
        for k in range(3):
            out_ref[:, pl.ds(place(way * (k + 1), halves(c, h)), ROWS)] = mine_ref(k, h)
            out_ref[:, pl.ds(place(-way * (k + 1), halves(1 - c, h)), ROWS)] = other_ref(k, h)
        far = place(4, halves(0, h))

        @pl.when(c == 0)
        def _():
            out_ref[:, pl.ds(far, ROWS)] = mine_ref(3, h)

        @pl.when(c == 1)
        def _():
            out_ref[:, pl.ds(far, ROWS)] = other_ref(3, h)


def contract(row_ref, places, stacks):
    total = None
    for (e, d), ref in zip(places, stacks):
        count = ref.shape[0] * ROWS
        at = (e * NY + d) * ROWS
        panel = ref[...].reshape(count, ref.shape[2])
        term = jnp.dot(row_ref[:, at : at + count], panel, preferred_element_type=F32)
        total = term if total is None else total + term
    return total


def square_kernel(places, own, mine, other, *refs):
    stacks, (row_ref, out_ref) = refs[: len(places)], refs[len(places) :]

    def half(h):
        return slice(h * ROWS, (h + 1) * ROWS)

    reorder(
        lambda h: own[:, half(h)],
        lambda k, h: mine[k, :, half(h)],
        lambda k, h: other[k, :, half(h)],
        row_ref,
        lambda core, h: h,
    )
    out_ref[...] = contract(row_ref, places, stacks).astype(BF16)


def single_kernel(places, row_ref, *refs):
    stacks, (out_ref,) = refs[: len(places)], refs[len(places) :]
    out_ref[...] = 3.0 * contract(row_ref, places, stacks)


def more_kernel(places, single, row_ref, *refs):
    stacks, (out_ref,) = refs[: len(places)], refs[len(places) :]
    out_ref[...] = single[...] + 3.0 * contract(row_ref, places, stacks)


def last_kernel(places, own, mine, other, single, *refs):
    stacks, (out_ref, squared_ref) = refs[: len(places)], refs[len(places) :]
    reorder(
        lambda h: own[h],
        lambda k, h: mine[k, h],
        lambda k, h: other[k, h],
        squared_ref,
        lambda core, h: core if h == 0 else 1 - core,
    )
    out_ref[...] = (single[...] - 2.0 * contract(squared_ref, places, stacks)).astype(BF16)


def call(kernel, parts, scratch, out_shape, flops, *operands):
    operands += tuple(blocks for _, blocks in parts)
    vmem = pl.BlockSpec(memory_space=pltpu.VMEM)
    return pl.pallas_call(
        functools.partial(kernel, [place for place, _ in parts]),
        out_shape=out_shape,
        in_specs=[vmem] * len(operands),
        out_specs=jax.tree.map(lambda _: vmem, out_shape),
        scratch_shapes=scratch,
        compiler_params=pltpu.CompilerParams(vmem_limit_bytes=16 * 1024 * 1024),
        cost_estimate=pl.CostEstimate(flops=flops, bytes_accessed=1 << 20, transcendentals=0),
    )(*operands)


def shards(density, panel, pattern):
    panel_f32 = jax.ShapeDtypeStruct((ROWS, WIDTH), F32)
    row_bf16 = jax.ShapeDtypeStruct((ROWS, DEPTH), BF16)
    core = lax.axis_index("c")
    mask = pattern.astype(BF16)
    filtered = (
        density.reshape(ROWS // BS, BS, INNER // BS, BS) * mask[:, None, :, None]
    ).reshape(ROWS, INNER)
    own_columns = lax.dynamic_slice_in_dim(filtered, core * PART, PART, 1)
    own_panel = lax.dynamic_slice_in_dim(panel, core * WIDTH, WIDTH, 1)

    both = jnp.concatenate([own_columns, own_panel], 1)
    both_one, both_three = first(both, 1), first(both, 3)
    columns_two = first(own_columns, 2)
    one_on, two_on = along(filtered, 1), along(filtered, 2)
    near_columns = joined([own_columns, both_one[:, :PART], columns_two, both_three[:, :PART]])

    near_columns = after(near_columns, one_on, two_on)
    pair = after(joined([one_on, two_on]), both_one, both_three, columns_two)
    panel_two = first(after(own_panel, one_on), 2)
    near_panel = joined([own_panel, both_one[:, PART:], panel_two, both_three[:, PART:]])
    columns = [near_columns] + [second(near_columns, e) for e in (1, 2, 3)]
    filtered_mine = jnp.concatenate([pair, along(pair, 2)], 0)
    filtered_mine = after(filtered_mine, *columns[1:])
    filtered_line = (filtered, filtered_mine, swapped(filtered_mine))

    near_panel = after(near_panel, *columns[1:])
    plus, minus = second(near_panel, 1), second(near_panel, 3)
    row, squared = call(
        square_kernel,
        [((e, 0), blocks) for e, blocks in enumerate(columns)],
        [],
        (row_bf16, jax.ShapeDtypeStruct((ROWS, PART), BF16)),
        2 * ROWS * DEPTH * PART,
        *filtered_line,
    )
    squared = joined([squared, swapped(squared)])
    one_on, two_on = along(squared, 1), along(squared, 2)
    squared_mine = joined([one_on, two_on, *farther(two_on)])
    squared_mine = after(squared_mine, plus, minus)
    squared_line = (squared, squared_mine, swapped(squared_mine))
    early = [((0, 0), near_panel), ((1, 0), plus), ((3, 0), minus)]
    late = [((2, 0), second(plus[:2], 1)), ((2, 2), second(minus[2:], 3))]
    flops = 2 * ROWS * DEPTH * WIDTH
    single = call(single_kernel, early, [], panel_f32, flops // 64, row)
    single = call(more_kernel, late, [], panel_f32, flops, single, row)
    return call(
        last_kernel,
        early + late,
        [pltpu.VMEM((ROWS, DEPTH), BF16)],
        jax.ShapeDtypeStruct((ROWS, WIDTH), BF16),
        flops,
        *squared_line,
        single,
    )


def solution(mesh):
    fine = Mesh(mesh.devices.reshape(NY, NX, NZ, NC), AXES)
    rows = ("y", "x")
    return jax.shard_map(
        shards,
        mesh=fine,
        in_specs=(P(rows, "z"), P(rows, "z"), P(rows, "z")),
        out_specs=P(rows, ("z", "c")),
        check_vma=False,
    )
```

```python
import functools

import jax
import jax.numpy as jnp
from jax import lax
from jax.experimental import pallas as pl
from jax.experimental.pallas import tpu as pltpu
from jax.sharding import Mesh, PartitionSpec as P

BS = 128
NY, NX, NZ, NC = 4, 4, 8, 2
ROWS, INNER, WIDTH = 256, 512, 1024
PART = INNER // NC
DEPTH = NY * NX * ROWS
AXES = ("y", "x", "z", "c")
BF16, F32 = jnp.bfloat16, jnp.float32


def moved(block, source_of):
    def index(y, x, z, c):
        return ((y * NX + x) * NZ + z) * NC + c

    route = []
    for y in range(NY):
        for x in range(NX):
            for z in range(NZ):
                for c in range(NC):
                    source = source_of(y, x, z, c)
                    if source is not None:
                        route.append((index(*source), index(y, x, z, c)))
    return lax.ppermute(block, AXES, route)


def first(block, step):
    return moved(
        block,
        lambda y, x, z, c: ((y + step) % NY, x, z, c) if c == 0 else (y, (x + step) % NX, z, c),
    )


def second(block, step):
    return moved(
        block,
        lambda y, x, z, c: (y, (x + step) % NX, z, c) if c == 0 else ((y + step) % NY, x, z, c),
    )


def swapped(block):
    return moved(block, lambda y, x, z, c: (y, x, z, 1 - c))


def along(block, step):
    return moved(block, lambda y, x, z, c: (y, x, (z + (step if c == 0 else -step)) % NZ, c))


def joined(blocks):
    return jnp.stack(blocks)


def after(value, *others):
    return lax.optimization_barrier((value, others))[0]


def farther(two_on):
    four = moved(two_on, lambda y, x, z, c: (y, x, (z + 2) % NZ, c) if c == 0 else None)
    return along(two_on, 1), four


def positions():
    y, x, z, c = (lax.axis_index(name) for name in AXES)

    def place(offset, half):
        block = 2 * ((z + offset + NZ) % NZ) + half
        down, right = (block // NX - y + NY) % NY, (block % NX - x + NX) % NX
        d = jnp.where(c == 0, down, right)
        e = jnp.where(c == 0, right, down)
        return pl.multiple_of((e * NY + d) * ROWS, ROWS)

    return c, place


def reorder(own_ref, mine_ref, other_ref, out_ref, halves):
    c, place = positions()
    way = 1 - 2 * c
    for h in range(2):
        out_ref[:, pl.ds(place(0, halves(c, h)), ROWS)] = own_ref(h)
        for k in range(3):
            out_ref[:, pl.ds(place(way * (k + 1), halves(c, h)), ROWS)] = mine_ref(k, h)
            out_ref[:, pl.ds(place(-way * (k + 1), halves(1 - c, h)), ROWS)] = other_ref(k, h)
        far = place(4, halves(0, h))

        @pl.when(c == 0)
        def _():
            out_ref[:, pl.ds(far, ROWS)] = mine_ref(3, h)

        @pl.when(c == 1)
        def _():
            out_ref[:, pl.ds(far, ROWS)] = other_ref(3, h)


def contract(row_ref, places, stacks):
    total = None
    for (e, d), ref in zip(places, stacks):
        count = ref.shape[0] * ROWS
        at = (e * NY + d) * ROWS
        panel = ref[...].reshape(count, ref.shape[2])
        term = jnp.dot(row_ref[:, at : at + count], panel, preferred_element_type=F32)
        total = term if total is None else total + term
    return total


def square_kernel(places, own, mine, other, *refs):
    stacks, (row_ref, out_ref) = refs[: len(places)], refs[len(places) :]

    def half(h):
        return slice(h * ROWS, (h + 1) * ROWS)

    reorder(
        lambda h: own[:, half(h)],
        lambda k, h: mine[k, :, half(h)],
        lambda k, h: other[k, :, half(h)],
        row_ref,
        lambda core, h: h,
    )
    out_ref[...] = contract(row_ref, places, stacks).astype(BF16)


def single_kernel(places, row_ref, *refs):
    stacks, (out_ref,) = refs[: len(places)], refs[len(places) :]
    out_ref[...] = 3.0 * contract(row_ref, places, stacks)


def double_kernel(places, own, mine, far, other, other_far, single, *refs):
    stacks, (row_ref, out_ref) = refs[: len(places)], refs[len(places) :]

    def read(near, beyond):
        return lambda k, h: near[k, h] if k < 2 else beyond[k - 2, h]

    reorder(
        lambda h: own[h],
        read(mine, far),
        read(other, other_far),
        row_ref,
        lambda core, h: core if h == 0 else 1 - core,
    )
    out_ref[...] = single[...] - 2.0 * contract(row_ref, places, stacks)


def last_kernel(places, row_ref, squared_ref, total, *refs):
    stacks, (out_ref,) = refs[: len(places)], refs[len(places) :]
    once = contract(row_ref, places, stacks)
    twice = contract(squared_ref, places, stacks)
    out_ref[...] = (total[...] + (3.0 * once - 2.0 * twice)).astype(BF16)


def call(kernel, parts, scratch, out_shape, flops, *operands):
    operands += tuple(blocks for _, blocks in parts)
    vmem = pl.BlockSpec(memory_space=pltpu.VMEM)
    return pl.pallas_call(
        functools.partial(kernel, [place for place, _ in parts]),
        out_shape=out_shape,
        in_specs=[vmem] * len(operands),
        out_specs=jax.tree.map(lambda _: vmem, out_shape),
        scratch_shapes=scratch,
        compiler_params=pltpu.CompilerParams(vmem_limit_bytes=16 * 1024 * 1024),
        cost_estimate=pl.CostEstimate(flops=flops, bytes_accessed=1 << 20, transcendentals=0),
    )(*operands)


def shards(density, panel, pattern):
    panel_f32 = jax.ShapeDtypeStruct((ROWS, WIDTH), F32)
    row_bf16 = jax.ShapeDtypeStruct((ROWS, DEPTH), BF16)
    core = lax.axis_index("c")
    mask = pattern.astype(BF16)
    filtered = (
        density.reshape(ROWS // BS, BS, INNER // BS, BS) * mask[:, None, :, None]
    ).reshape(ROWS, INNER)
    own_columns = lax.dynamic_slice_in_dim(filtered, core * PART, PART, 1)
    own_panel = lax.dynamic_slice_in_dim(panel, core * WIDTH, WIDTH, 1)

    both = jnp.concatenate([own_columns, own_panel], 1)
    both_one, both_three = first(both, 1), first(both, 3)
    columns_two = first(own_columns, 2)
    one_on, two_on = along(filtered, 1), along(filtered, 2)
    near_columns = joined([own_columns, both_one[:, :PART], columns_two, both_three[:, :PART]])

    near_columns = after(near_columns, one_on, two_on)
    pair = after(joined([one_on, two_on]), both_one, both_three, columns_two)
    panel_two = first(after(own_panel, one_on), 2)
    near_panel = joined([own_panel, both_one[:, PART:], panel_two, both_three[:, PART:]])
    columns = [near_columns] + [second(near_columns, e) for e in (1, 2, 3)]
    filtered_mine = jnp.concatenate([pair, along(pair, 2)], 0)
    filtered_mine = after(filtered_mine, *columns[1:])
    filtered_line = (filtered, filtered_mine, swapped(filtered_mine))

    plus = second(after(near_panel, columns[1], columns[2]), 1)
    minus = second(after(near_panel, *columns[1:]), 3)
    row, squared = call(
        square_kernel,
        [((e, 0), blocks) for e, blocks in enumerate(columns)],
        [],
        (row_bf16, jax.ShapeDtypeStruct((ROWS, PART), BF16)),
        2 * ROWS * DEPTH * PART,
        *filtered_line,
    )
    squared = joined([squared, swapped(squared)])
    one_on, two_on = along(squared, 1), along(squared, 2)
    mine = joined([one_on, two_on])
    far = joined(list(farther(two_on)))
    early = [((0, 0), near_panel), ((1, 0), plus), ((3, 0), minus)]
    plus_part = after(plus[:2], one_on, two_on)
    late = [((2, 0), second(plus_part, 1)), ((2, 2), second(minus[2:], 3))]
    flops = 2 * ROWS * DEPTH * WIDTH
    single = call(single_kernel, early, [], panel_f32, flops, row)
    squared_row, total = call(
        double_kernel,
        early,
        [],
        (row_bf16, panel_f32),
        flops // 1,
        squared,
        mine,
        far,
        swapped(mine),
        swapped(far),
        single,
    )
    return call(
        last_kernel,
        late,
        [],
        jax.ShapeDtypeStruct((ROWS, WIDTH), BF16),
        flops // 64,
        row,
        squared_row,
        total,
    )


def solution(mesh):
    fine = Mesh(mesh.devices.reshape(NY, NX, NZ, NC), AXES)
    rows = ("y", "x")
    return jax.shard_map(
        shards,
        mesh=fine,
        in_specs=(P(rows, "z"), P(rows, "z"), P(rows, "z")),
        out_specs=P(rows, ("z", "c")),
        check_vma=False,
    )
```

```python
import functools

import jax
import jax.numpy as jnp
from jax import lax
from jax.experimental import pallas as pl
from jax.experimental.pallas import tpu as pltpu
from jax.sharding import Mesh, PartitionSpec as P

BS = 128
NY, NX, NZ, NC = 4, 4, 8, 2
ROWS, INNER, WIDTH = 256, 512, 1024
PART = INNER // NC
DEPTH = NY * NX * ROWS
AXES = ("y", "x", "z", "c")
BF16, F32 = jnp.bfloat16, jnp.float32


def moved(block, source_of):
    def index(y, x, z, c):
        return ((y * NX + x) * NZ + z) * NC + c

    route = []
    for y in range(NY):
        for x in range(NX):
            for z in range(NZ):
                for c in range(NC):
                    source = source_of(y, x, z, c)
                    if source is not None:
                        route.append((index(*source), index(y, x, z, c)))
    return lax.ppermute(block, AXES, route)


def first(block, step):
    return moved(
        block,
        lambda y, x, z, c: ((y + step) % NY, x, z, c) if c == 0 else (y, (x + step) % NX, z, c),
    )


def second(block, step):
    return moved(
        block,
        lambda y, x, z, c: (y, (x + step) % NX, z, c) if c == 0 else ((y + step) % NY, x, z, c),
    )


def swapped(block):
    return moved(block, lambda y, x, z, c: (y, x, z, 1 - c))


def along(block, step):
    return moved(block, lambda y, x, z, c: (y, x, (z + (step if c == 0 else -step)) % NZ, c))


def joined(blocks):
    return jnp.stack(blocks)


def after(value, *others):
    return lax.optimization_barrier((value, others))[0]


def farther(two_on):
    four = moved(two_on, lambda y, x, z, c: (y, x, (z + 2) % NZ, c) if c == 0 else None)
    return along(two_on, 1), four


def positions():
    y, x, z, c = (lax.axis_index(name) for name in AXES)

    def place(offset, half):
        block = 2 * ((z + offset + NZ) % NZ) + half
        down, right = (block // NX - y + NY) % NY, (block % NX - x + NX) % NX
        d = jnp.where(c == 0, down, right)
        e = jnp.where(c == 0, right, down)
        return pl.multiple_of((e * NY + d) * ROWS, ROWS)

    return c, place


def reorder(own_ref, mine_ref, other_ref, out_ref, halves):
    c, place = positions()
    way = 1 - 2 * c
    for h in range(2):
        out_ref[:, pl.ds(place(0, halves(c, h)), ROWS)] = own_ref(h)
        for k in range(3):
            out_ref[:, pl.ds(place(way * (k + 1), halves(c, h)), ROWS)] = mine_ref(k, h)
            out_ref[:, pl.ds(place(-way * (k + 1), halves(1 - c, h)), ROWS)] = other_ref(k, h)
        far = place(4, halves(0, h))

        @pl.when(c == 0)
        def _():
            out_ref[:, pl.ds(far, ROWS)] = mine_ref(3, h)

        @pl.when(c == 1)
        def _():
            out_ref[:, pl.ds(far, ROWS)] = other_ref(3, h)


def contract(row_ref, places, stacks):
    total = None
    for (e, d), ref in zip(places, stacks):
        count = ref.shape[0] * ROWS
        at = (e * NY + d) * ROWS
        panel = ref[...].reshape(count, ref.shape[2])
        term = jnp.dot(row_ref[:, at : at + count], panel, preferred_element_type=F32)
        total = term if total is None else total + term
    return total


def square_kernel(places, own, mine, other, *refs):
    stacks, (row_ref, out_ref) = refs[: len(places)], refs[len(places) :]

    def half(h):
        return slice(h * ROWS, (h + 1) * ROWS)

    reorder(
        lambda h: own[:, half(h)],
        lambda k, h: mine[k, :, half(h)],
        lambda k, h: other[k, :, half(h)],
        row_ref,
        lambda core, h: h,
    )
    out_ref[...] = contract(row_ref, places, stacks).astype(BF16)


def single_kernel(places, row_ref, *refs):
    stacks, (out_ref,) = refs[: len(places)], refs[len(places) :]
    out_ref[...] = 3.0 * contract(row_ref, places, stacks)


def double_kernel(places, own, mine, far, other, other_far, single, *refs):
    stacks, (row_ref, out_ref) = refs[: len(places)], refs[len(places) :]

    def read(near, beyond):
        return lambda k, h: near[k, h] if k < 2 else beyond[k - 2, h]

    reorder(
        lambda h: own[h],
        read(mine, far),
        read(other, other_far),
        row_ref,
        lambda core, h: core if h == 0 else 1 - core,
    )
    out_ref[...] = single[...] - 2.0 * contract(row_ref, places, stacks)


def last_kernel(places, row_ref, squared_ref, total, *refs):
    stacks, (out_ref,) = refs[: len(places)], refs[len(places) :]
    once = contract(row_ref, places, stacks)
    twice = contract(squared_ref, places, stacks)
    out_ref[...] = (total[...] + (3.0 * once - 2.0 * twice)).astype(out_ref.dtype)


def call(kernel, parts, scratch, out_shape, flops, *operands):
    operands += tuple(blocks for _, blocks in parts)
    vmem = pl.BlockSpec(memory_space=pltpu.VMEM)
    return pl.pallas_call(
        functools.partial(kernel, [place for place, _ in parts]),
        out_shape=out_shape,
        in_specs=[vmem] * len(operands),
        out_specs=jax.tree.map(lambda _: vmem, out_shape),
        scratch_shapes=scratch,
        compiler_params=pltpu.CompilerParams(vmem_limit_bytes=16 * 1024 * 1024),
        cost_estimate=pl.CostEstimate(flops=flops, bytes_accessed=1 << 20, transcendentals=0),
    )(*operands)


def shards(density, panel, pattern):
    panel_f32 = jax.ShapeDtypeStruct((ROWS, WIDTH), F32)
    row_bf16 = jax.ShapeDtypeStruct((ROWS, DEPTH), BF16)
    core = lax.axis_index("c")
    mask = pattern.astype(BF16)
    filtered = (
        density.reshape(ROWS // BS, BS, INNER // BS, BS) * mask[:, None, :, None]
    ).reshape(ROWS, INNER)
    own_columns = lax.dynamic_slice_in_dim(filtered, core * PART, PART, 1)
    own_panel = lax.dynamic_slice_in_dim(panel, core * WIDTH, WIDTH, 1)

    both = jnp.concatenate([own_columns, own_panel], 1)
    both_one, both_three = first(both, 1), first(both, 3)
    columns_two = first(own_columns, 2)
    one_on, two_on = along(filtered, 1), along(filtered, 2)
    near_columns = joined([own_columns, both_one[:, :PART], columns_two, both_three[:, :PART]])

    near_columns = after(near_columns, one_on, two_on)
    pair = after(joined([one_on, two_on]), both_one, both_three, columns_two)
    panel_two = first(after(own_panel, one_on), 2)
    near_panel = joined([own_panel, both_one[:, PART:], panel_two, both_three[:, PART:]])
    columns = [near_columns] + [second(near_columns, e) for e in (1, 3, 2)]
    filtered_mine = jnp.concatenate([pair, along(pair, 2)], 0)
    filtered_mine = after(filtered_mine, *columns[1:])
    filtered_line = (filtered, filtered_mine, swapped(filtered_mine))

    plus = second(after(near_panel, columns[1], columns[2]), 1)
    minus = second(after(near_panel, *columns[1:]), 3)
    row, squared = call(
        square_kernel,
        [((e, 0), blocks) for e, blocks in zip((0, 1, 3, 2), columns)],
        [],
        (row_bf16, jax.ShapeDtypeStruct((ROWS, PART), BF16)),
        2 * ROWS * DEPTH * PART,
        *filtered_line,
    )
    squared = joined([squared, swapped(squared)])
    one_on, two_on = along(squared, 1), along(squared, 2)
    mine = joined([one_on, two_on])
    far = joined(list(farther(two_on)))
    early = [((0, 0), near_panel), ((1, 0), plus), ((3, 0), minus)]
    plus_part = after(plus[:2], one_on, two_on)
    late = [((2, 0), second(plus_part, 1)), ((2, 2), second(minus[2:], 3))]
    flops = 2 * ROWS * DEPTH * WIDTH
    single = call(single_kernel, early, [], panel_f32, flops, row)
    squared_row, total = call(
        double_kernel,
        early,
        [],
        (row_bf16, panel_f32),
        flops // 1,
        squared,
        mine,
        far,
        swapped(mine),
        swapped(far),
        single,
    )
    total = call(last_kernel, late[:1], [], panel_f32, flops // 64, row, squared_row, total)
    return call(
        last_kernel,
        late[1:],
        [],
        jax.ShapeDtypeStruct((ROWS, WIDTH), BF16),
        flops // 64,
        row,
        squared_row,
        total,
    )


def solution(mesh):
    fine = Mesh(mesh.devices.reshape(NY, NX, NZ, NC), AXES)
    rows = ("y", "x")
    return jax.shard_map(
        shards,
        mesh=fine,
        in_specs=(P(rows, "z"), P(rows, "z"), P(rows, "z")),
        out_specs=P(rows, ("z", "c")),
        check_vma=False,
    )
```

```python
import functools

import jax
import jax.numpy as jnp
from jax import lax
from jax.experimental import pallas as pl
from jax.experimental.pallas import tpu as pltpu
from jax.sharding import Mesh, PartitionSpec as P

BS = 128
NY, NX, NZ, NC = 4, 4, 8, 2
ROWS, INNER, WIDTH = 256, 512, 1024
PART = INNER // NC
DEPTH = NY * NX * ROWS
AXES = ("y", "x", "z", "c")
BF16, F32 = jnp.bfloat16, jnp.float32


def moved(block, source_of):
    def index(y, x, z, c):
        return ((y * NX + x) * NZ + z) * NC + c

    route = []
    for y in range(NY):
        for x in range(NX):
            for z in range(NZ):
                for c in range(NC):
                    source = source_of(y, x, z, c)
                    if source is not None:
                        route.append((index(*source), index(y, x, z, c)))
    return lax.ppermute(block, AXES, route)


def first(block, step):
    return moved(
        block,
        lambda y, x, z, c: ((y + step) % NY, x, z, c) if c == 0 else (y, (x + step) % NX, z, c),
    )


def second(block, step):
    return moved(
        block,
        lambda y, x, z, c: (y, (x + step) % NX, z, c) if c == 0 else ((y + step) % NY, x, z, c),
    )


def swapped(block):
    return moved(block, lambda y, x, z, c: (y, x, z, 1 - c))


def along(block, step):
    return moved(block, lambda y, x, z, c: (y, x, (z + (step if c == 0 else -step)) % NZ, c))


def joined(blocks):
    return jnp.stack(blocks)


def after(value, *others):
    return lax.optimization_barrier((value, others))[0]


def farther(two_on):
    four = moved(two_on, lambda y, x, z, c: (y, x, (z + 2) % NZ, c) if c == 0 else None)
    return along(two_on, 1), four


def positions():
    y, x, z, c = (lax.axis_index(name) for name in AXES)

    def place(offset, half):
        block = 2 * ((z + offset + NZ) % NZ) + half
        down, right = (block // NX - y + NY) % NY, (block % NX - x + NX) % NX
        d = jnp.where(c == 0, down, right)
        e = jnp.where(c == 0, right, down)
        return pl.multiple_of((e * NY + d) * ROWS, ROWS)

    return c, place


def reorder(own_ref, mine_ref, other_ref, out_ref, halves):
    c, place = positions()
    way = 1 - 2 * c
    for h in range(2):
        out_ref[:, pl.ds(place(0, halves(c, h)), ROWS)] = own_ref(h)
        for k in range(3):
            out_ref[:, pl.ds(place(way * (k + 1), halves(c, h)), ROWS)] = mine_ref(k, h)
            out_ref[:, pl.ds(place(-way * (k + 1), halves(1 - c, h)), ROWS)] = other_ref(k, h)
        far = place(4, halves(0, h))

        @pl.when(c == 0)
        def _():
            out_ref[:, pl.ds(far, ROWS)] = mine_ref(3, h)

        @pl.when(c == 1)
        def _():
            out_ref[:, pl.ds(far, ROWS)] = other_ref(3, h)


def contract(row_ref, places, stacks):
    total = None
    for (e, d), ref in zip(places, stacks):
        count = ref.shape[0] * ROWS
        at = (e * NY + d) * ROWS
        panel = ref[...].reshape(count, ref.shape[2])
        term = jnp.dot(row_ref[:, at : at + count], panel, preferred_element_type=F32)
        total = term if total is None else total + term
    return total


def square_kernel(places, own, mine, other, *refs):
    stacks, (row_ref, out_ref) = refs[: len(places)], refs[len(places) :]

    def half(h):
        return slice(h * ROWS, (h + 1) * ROWS)

    reorder(
        lambda h: own[:, half(h)],
        lambda k, h: mine[k, :, half(h)],
        lambda k, h: other[k, :, half(h)],
        row_ref,
        lambda core, h: h,
    )
    out_ref[...] = contract(row_ref, places, stacks).astype(BF16)


def single_kernel(places, row_ref, *refs):
    stacks, (out_ref,) = refs[: len(places)], refs[len(places) :]
    out_ref[...] = 3.0 * contract(row_ref, places, stacks)


def double_kernel(places, own, mine, far, other, other_far, single, *refs):
    stacks, (row_ref, out_ref) = refs[: len(places)], refs[len(places) :]

    def read(near, beyond):
        return lambda k, h: near[k, h] if k < 2 else beyond[k - 2, h]

    reorder(
        lambda h: own[h],
        read(mine, far),
        read(other, other_far),
        row_ref,
        lambda core, h: core if h == 0 else 1 - core,
    )
    out_ref[...] = single[...] - 2.0 * contract(row_ref, places, stacks)


def last_kernel(places, row_ref, squared_ref, total, *refs):
    stacks, (out_ref,) = refs[: len(places)], refs[len(places) :]
    once = contract(row_ref, places, stacks)
    twice = contract(squared_ref, places, stacks)
    out_ref[...] = (total[...] + (3.0 * once - 2.0 * twice)).astype(out_ref.dtype)


def call(kernel, parts, scratch, out_shape, flops, *operands):
    operands += tuple(blocks for _, blocks in parts)
    vmem = pl.BlockSpec(memory_space=pltpu.VMEM)
    return pl.pallas_call(
        functools.partial(kernel, [place for place, _ in parts]),
        out_shape=out_shape,
        in_specs=[vmem] * len(operands),
        out_specs=jax.tree.map(lambda _: vmem, out_shape),
        scratch_shapes=scratch,
        compiler_params=pltpu.CompilerParams(vmem_limit_bytes=16 * 1024 * 1024),
        cost_estimate=pl.CostEstimate(flops=flops, bytes_accessed=1 << 20, transcendentals=0),
    )(*operands)


def shards(density, panel, pattern):
    panel_f32 = jax.ShapeDtypeStruct((ROWS, WIDTH), F32)
    row_bf16 = jax.ShapeDtypeStruct((ROWS, DEPTH), BF16)
    core = lax.axis_index("c")
    mask = pattern.astype(BF16)
    filtered = (
        density.reshape(ROWS // BS, BS, INNER // BS, BS) * mask[:, None, :, None]
    ).reshape(ROWS, INNER)
    own_columns = lax.dynamic_slice_in_dim(filtered, core * PART, PART, 1)
    own_panel = lax.dynamic_slice_in_dim(panel, core * WIDTH, WIDTH, 1)

    both = jnp.concatenate([own_columns, own_panel], 1)
    both_one, both_three = first(both, 1), first(both, 3)
    columns_two = first(own_columns, 2)
    one_on, two_on = along(filtered, 1), along(filtered, 2)
    near_columns = joined([own_columns, both_one[:, :PART], columns_two, both_three[:, :PART]])

    near_columns = after(near_columns, one_on, two_on)
    pair = after(joined([one_on, two_on]), both_one, both_three, columns_two)
    panel_two = first(after(own_panel, one_on), 2)
    near_panel = joined([own_panel, both_one[:, PART:], panel_two, both_three[:, PART:]])
    columns = [near_columns] + [second(near_columns, e) for e in (1, 3, 2)]
    filtered_mine = jnp.concatenate([pair, along(pair, 2)], 0)
    filtered_mine = after(filtered_mine, *columns[1:])
    filtered_line = (filtered, filtered_mine, swapped(filtered_mine))

    plus = second(after(near_panel, columns[1], columns[2]), 1)
    minus = second(after(near_panel, *columns[1:]), 3)
    row, squared = call(
        square_kernel,
        [((e, 0), blocks) for e, blocks in zip((0, 1, 3, 2), columns)],
        [],
        (row_bf16, jax.ShapeDtypeStruct((ROWS, PART), BF16)),
        2 * ROWS * DEPTH * PART,
        *filtered_line,
    )
    squared = joined([squared, swapped(squared)])
    one_on, two_on = along(squared, 1), along(squared, 2)
    mine = joined([one_on, two_on])
    far = joined(list(farther(two_on)))
    early = [((0, 0), near_panel), ((1, 0), plus), ((3, 0), minus)]
    plus_part = after(plus[:2], one_on, two_on)
    late = [((2, 0), second(plus_part, 1)), ((2, 2), second(minus[2:], 3))]
    flops = 2 * ROWS * DEPTH * WIDTH
    single = call(single_kernel, early, [], panel_f32, flops, row)
    squared_row, total = call(
        double_kernel,
        early,
        [],
        (row_bf16, panel_f32),
        flops // 1,
        squared,
        mine,
        far,
        swapped(mine),
        swapped(after(far, single)),
        single,
    )
    total = call(last_kernel, late[:1], [], panel_f32, flops // 64, row, squared_row, total)
    return call(
        last_kernel,
        late[1:],
        [],
        jax.ShapeDtypeStruct((ROWS, WIDTH), BF16),
        flops // 64,
        row,
        squared_row,
        total,
    )


def solution(mesh):
    fine = Mesh(mesh.devices.reshape(NY, NX, NZ, NC), AXES)
    rows = ("y", "x")
    return jax.shard_map(
        shards,
        mesh=fine,
        in_specs=(P(rows, "z"), P(rows, "z"), P(rows, "z")),
        out_specs=P(rows, ("z", "c")),
        check_vma=False,
    )
```
